32 devices in a mesh: ang: 4 (over y, x), pix: 8 (over z, core).
Axes of the slice: x: 2, y: 2, z: 4, core: 2. Of those that a mesh axis runs over, the one named last changes fastest.
Arguments:
- flats: float32 [256, 64, 4096], P(None, 'pix', 'ang'), may hold values from -60 to 60
- projections: float32 [128, 64, 4096], P('ang', None, 'pix'), may hold values from -60 to 60
- start_basis: float32 [256, 48], replicated, may hold values from -0.375 to 0.375
Outputs:
- corrected: float32 [128, 64, 4096], P('ang', None, 'pix')
The draws below stay inside these ranges and needn't reach their ends.
All inputs are finite; a program needn't handle non-finite values.
Results may differ from the reference program's by a relative error of at most 0.0001.
Values sent between devices are 32-bit elements; how exact they have to be, the bound alone decides.
A program may use at most 128 MiB of HBM per device.

```python
import jax
import jax.numpy as jnp
from jax import lax

NF = 256
NEIG = 48
SUBSPACE = 2
ROWS = 64
COLS = 4096
NPROJ = 128


mode_count = 64


def base_field(key):
    key_base = jax.random.fold_in(key, 101)
    rows = jnp.arange(ROWS, dtype=jnp.float32) / ROWS
    ramp = 0.5 + rows
    rough = jnp.exp(jax.random.uniform(key_base, (ROWS, COLS), jnp.float32, -0.4, 0.4))
    return ramp[:, None] * rough


def shaped(key, amps):
    key_modes = jax.random.fold_in(key, 202)

    def add_mode(index, total):
        field = 0.12 * jax.random.truncated_normal(jax.random.fold_in(key_modes, index), -3.0, 3.0, (ROWS, COLS), jnp.float32)
        decay = lax.rsqrt(1.0 + index.astype(jnp.float32))
        column = lax.dynamic_index_in_dim(amps, index, 1, keepdims=False) * decay
        return total + column[:, None, None] * field[None]
    start = jnp.ones((amps.shape[0], ROWS, COLS), jnp.float32)
    total = lax.fori_loop(0, mode_count, add_mode, start)
    return base_field(key)[None] * total


def draw_flats(key, part):
    amps = jax.random.truncated_normal(jax.random.fold_in(key, 303), -3.0, 3.0, (NF, mode_count), jnp.float32)
    key_noise = jax.random.fold_in(key, 404)
    noise = 0.005 * jax.random.truncated_normal(key_noise, -4.0, 4.0, (NF, ROWS, COLS), jnp.float32)
    return shaped(key, amps) + noise


def draw_projections(key, part):
    amps = jax.random.truncated_normal(jax.random.fold_in(key, 505), -3.0, 3.0, (NPROJ, mode_count), jnp.float32)
    sample = jax.random.uniform(jax.random.fold_in(key, 606), (NPROJ, ROWS, COLS), jnp.float32, 0.3, 1.0)
    key_noise = jax.random.fold_in(key, 707)
    noise = 0.02 * jax.random.truncated_normal(key_noise, -4.0, 4.0, (NPROJ, ROWS, COLS), jnp.float32)
    return shaped(key, amps) * sample + noise


def centred(key, shape, spread, limit, held_as=jnp.bfloat16):
    array = jax.random.normal(key, shape, jnp.float32) * spread
    return jnp.minimum(jnp.maximum(array, -limit), limit).astype(held_as)


def setup_inputs(seed: int = 0) -> dict:
    splits = jax.random.split(jax.random.key(seed), 4)
    flats = draw_flats(jax.random.fold_in(splits[3], 71), 0)
    projections = draw_projections(jax.random.fold_in(splits[3], 71), 0)
    start_basis = centred(splits[2], (NF, NEIG), NF ** -0.5, 0.375, jnp.float32)
    return {"flats": flats, "projections": projections, "start_basis": start_basis}


floor_value = 0.2

def factor_lower(matrix):
    order = matrix.shape[0]
    places = jnp.arange(order)

    def add_column(index, lower):
        pick = (places == index).astype(matrix.dtype)
        before = (places < index).astype(matrix.dtype)
        row_now = jnp.dot(pick, lower, precision=lax.Precision.HIGHEST) * before
        column = jnp.dot(matrix, pick, precision=lax.Precision.HIGHEST)
        pivot = jnp.sqrt(jnp.sum(column * pick) - jnp.sum(row_now * row_now))
        below = (column - jnp.dot(lower, row_now, precision=lax.Precision.HIGHEST)) / pivot
        fresh = jnp.where(places > index, below, jnp.zeros_like(below)) + pick * pivot
        return lower + fresh[:, None] * pick[None, :]
    return lax.fori_loop(0, order, add_column, jnp.zeros_like(matrix))

def solve_lower(lower, target):
    order = lower.shape[0]
    places = jnp.arange(order)

    def forward(index, solved):
        pick = (places == index).astype(lower.dtype)
        row_now = jnp.dot(pick, lower, precision=lax.Precision.HIGHEST)
        pivot = jnp.sum(row_now * pick)
        row_off = row_now * (places < index).astype(lower.dtype)
        value = (jnp.dot(pick, target, precision=lax.Precision.HIGHEST) - jnp.dot(row_off, solved, precision=lax.Precision.HIGHEST)) / pivot
        return solved + pick[:, None] * value[None, :]
    return lax.fori_loop(0, order, forward, jnp.zeros_like(target))

def solve_upper(lower, target):
    order = lower.shape[0]
    places = jnp.arange(order)

    def backward(turn, solved):
        index = order - 1 - turn
        pick = (places == index).astype(lower.dtype)
        row_now = jnp.dot(lower, pick, precision=lax.Precision.HIGHEST)
        pivot = jnp.sum(row_now * pick)
        row_off = row_now * (places > index).astype(lower.dtype)
        value = (jnp.dot(pick, target, precision=lax.Precision.HIGHEST) - jnp.dot(row_off, solved, precision=lax.Precision.HIGHEST)) / pivot
        return solved + pick[:, None] * value[None, :]
    return lax.fori_loop(0, order, backward, jnp.zeros_like(target))

def orthonormal(grown):
    correlation = jnp.dot(grown.T, grown, precision=lax.Precision.HIGHEST)
    lower = factor_lower(correlation)
    return solve_lower(lower, grown.T).T

def solve_normal(normal, fit_rhs):
    factor = factor_lower(normal)
    inner = solve_lower(factor, fit_rhs.T)
    return solve_upper(factor, inner).T

def reference(flats, projections, start_basis):
    npix = flats.shape[1] * flats.shape[2]
    mean_flat = lax.optimization_barrier(jnp.mean(flats, axis=0))
    centered = (flats - mean_flat).reshape(flats.shape[0], -1)
    gram = jnp.dot(centered, centered.T, precision=lax.Precision.HIGHEST) / npix
    basis = start_basis
    for turn in range(SUBSPACE):
        basis = orthonormal(jnp.dot(gram, basis, precision=lax.Precision.HIGHEST))
    eigen_flats = jnp.dot(basis.T, centered, precision=lax.Precision.HIGHEST)
    normal = jnp.dot(basis.T, jnp.dot(gram, basis, precision=lax.Precision.HIGHEST), precision=lax.Precision.HIGHEST)
    flat_row = mean_flat.reshape(1, -1)
    frames = projections.reshape(projections.shape[0], -1)
    fit_rhs = jnp.dot(frames - flat_row, eigen_flats.T, precision=lax.Precision.HIGHEST) / npix
    weights = solve_normal(normal, fit_rhs)
    estimate = flat_row + jnp.dot(weights, eigen_flats, precision=lax.Precision.HIGHEST)
    corrected = frames / jnp.maximum(estimate, floor_value)
    return corrected.reshape(projections.shape)
```

```python
import functools

import jax
import jax.numpy as jnp
from jax import lax
from jax.experimental import pallas as pl
from jax.experimental.pallas import tpu as pltpu
from jax.sharding import PartitionSpec as P

SUBSPACE = 2
MESH = pl.DeviceIdType.MESH
HIGHEST = lax.Precision.HIGHEST
VMEM_LIMIT = 56 * 1024 * 1024

floor_value = 0.2


def dot_nt(a, b, precision=None):
    return lax.dot_general(
        a, b, (((1,), (1,)), ((), ())), precision=precision, preferred_element_type=jnp.float32
    )


def split(x):
    high = x.astype(jnp.bfloat16)
    low = (x - high.astype(jnp.float32)).astype(jnp.bfloat16)
    return high, low


def greet(ang, pix, a, p):
    barrier = pltpu.get_barrier_semaphore()
    for d in range(1, ang):
        pl.semaphore_signal(
            barrier, inc=1, device_id=(lax.rem(a + d, ang), p), device_id_type=MESH
        )
    for e in range(1, pix):
        pl.semaphore_signal(
            barrier, inc=1, device_id=(a, lax.rem(p + e, pix)), device_id_type=MESH
        )


def await_greetings(ang, pix):
    pl.semaphore_wait(pltpu.get_barrier_semaphore(), ang + pix - 2)


def send(src, dst, send_sem, recv_sem, device):
    copy = pltpu.make_async_remote_copy(
        src_ref=src, dst_ref=dst, send_sem=send_sem, recv_sem=recv_sem,
        device_id=device, device_id_type=MESH,
    )
    copy.start()
    return copy


LANES = 128


def load_strips(source, target, sems):
    copies = []
    for c in range(target.shape[0]):
        copy = pltpu.make_async_copy(
            source.at[:, pl.ds(c * LANES, LANES)], target.at[c], sems.at[c]
        )
        copy.start()
        copies.append(copy)
    return copies


def strided_row(strips, first, count, stride, group):
    return jnp.concatenate(
        [strips[c, pl.ds(first, count, stride=stride), :] for c in group], axis=1
    )


def gram_kernel(ang, pix, frames, rows, reduce_here, flats, gram, x, acc, cross, total,
                from_ang, from_pix, load_sem, s1, r1, s2, r2, s3, r3, s4, r4):
    a, p = lax.axis_index("ang"), lax.axis_index("pix")
    if reduce_here:
        greet(ang, pix, a, p)
    copies = load_strips(flats, x, load_sem)
    acc[...] = jnp.zeros_like(acc)
    cross[...] = jnp.zeros_like(cross)
    for c in range(0, len(copies), 2):
        copies[c].wait()
        copies[c + 1].wait()

        def one_row(r, carry):
            here = strided_row(x, r, frames, rows, (c, c + 1))
            high, low = split(here - jnp.mean(here, axis=0, keepdims=True))
            acc[...] += dot_nt(high, high)
            cross[...] += dot_nt(high, low)
            return carry
        lax.fori_loop(0, rows, one_row, 0)
    both = cross[...]
    acc[...] += both + both.T
    if not reduce_here:
        gram[...] = acc[...]
        return
    await_greetings(ang, pix)
    block = frames // ang
    piece = block // pix
    first = []
    for d in range(1, ang):
        x_to = lax.rem(a + d, ang)
        first.append(send(acc.at[pl.ds(pl.multiple_of(x_to * block, block), block)],
                          from_ang.at[d], s1.at[d], r1.at[d], (x_to, p)))
    mine = acc[pl.ds(pl.multiple_of(a * block, block), block), :]
    for copy in first:
        copy.wait_recv()
    for d in range(1, ang):
        mine = mine + from_ang[d]
    from_ang[0] = mine
    second = []
    for e in range(1, pix):
        q = lax.rem(p + e, pix)
        second.append(send(from_ang.at[0, pl.ds(pl.multiple_of(q * piece, piece), piece)],
                           from_pix.at[e], s2.at[e], r2.at[e], (a, q)))
    own = from_ang[0, pl.ds(pl.multiple_of(p * piece, piece), piece), :]
    for copy in second:
        copy.wait_recv()
    for e in range(1, pix):
        own = own + from_pix[e]
    at = pl.ds(pl.multiple_of(a * block + p * piece, piece), piece)
    total[at, :] = own
    third = []
    for e in range(1, pix):
        q = lax.rem(p + e, pix)
        third.append(send(total.at[at], total.at[at], s3.at[e], r3.at[e], (a, q)))
    for copy in third:
        copy.wait_recv()
    at = pl.ds(pl.multiple_of(a * block, block), block)
    fourth = []
    for d in range(1, ang):
        x_to = lax.rem(a + d, ang)
        fourth.append(send(total.at[at], total.at[at], s4.at[d], r4.at[d], (x_to, p)))
    for copy in fourth:
        copy.wait_recv()
    gram[...] = total[...]
    for copy in first + second + third + fourth:
        copy.wait_send()


def gram_of(flats, ang, pix):
    frames, rows, cols = flats.shape
    reduce_here = frames % (ang * pix * 8) == 0
    block, piece = frames // ang, max(8, frames // ang // pix)
    vmem, dma = pltpu.VMEM, pltpu.SemaphoreType.DMA
    gram = pl.pallas_call(
        functools.partial(gram_kernel, ang, pix, frames, rows, reduce_here),
        out_shape=jax.ShapeDtypeStruct((frames, frames), jnp.float32),
        in_specs=[pl.BlockSpec(memory_space=pl.ANY)],
        out_specs=pl.BlockSpec(memory_space=vmem),
        scratch_shapes=[
            vmem((cols // LANES, frames * rows, LANES), jnp.float32),
            vmem((frames, frames), jnp.float32),
            vmem((frames, frames), jnp.float32),
            vmem((frames, frames), jnp.float32),
            vmem((ang, block, frames), jnp.float32),
            vmem((pix, piece, frames), jnp.float32),
            dma((cols // LANES,)),
            dma((ang,)), dma((ang,)), dma((pix,)), dma((pix,)),
            dma((pix,)), dma((pix,)), dma((ang,)), dma((ang,)),
        ],
        compiler_params=pltpu.CompilerParams(
            collective_id=0 if reduce_here else None,
            has_side_effects=reduce_here, vmem_limit_bytes=VMEM_LIMIT,
        ),
        name="gram",
    )(flats.reshape(frames * rows, cols))
    return gram if reduce_here else lax.psum(gram, ("ang", "pix"))


def correct_kernel(ang, pix, frames, rows, angles, all_rows, modes, npix,
                   flats, projections, basis_t, solver, out,
                   x, proj, done, e_own, e_rows, e_all, fit, part, parts,
                   load_sem, proj_sem, out_sem, keep_sem, s1, r1, s2, r2, s3, r3, s4, r4):
    a, p = lax.axis_index("ang"), lax.axis_index("pix")
    greet(ang, pix, a, p)
    copies = load_strips(flats, x, load_sem)
    proj_copies = load_strips(projections, proj, proj_sem)
    quarter = rows // ang
    strips = proj.shape[0]
    wide = strips * LANES
    share = pix // ang
    e_own[...] = jnp.zeros_like(e_own)
    fit[...] = jnp.zeros_like(fit)
    b_high, b_low = split(basis_t[...])
    b_both = jnp.concatenate([b_high, b_low], axis=0)
    for copy in copies:
        copy.wait()

    def eigen_rows(x_to):
        for c in range(0, len(copies), 2):
            cut = pl.ds(c * LANES, 2 * LANES)
            for i in range(quarter):
                here = strided_row(x, x_to * quarter + i, frames, rows, (c, c + 1))
                mean = jnp.mean(here, axis=0, keepdims=True)
                high, low = split(here - mean)
                one = jnp.dot(b_both, high, preferred_element_type=jnp.float32)
                two = jnp.dot(b_high, low, preferred_element_type=jnp.float32)
                e_own[x_to, i * modes:(i + 1) * modes, cut] = one[:modes] + one[modes:] + two
                e_own[x_to, quarter * modes + i:quarter * modes + i + 1, cut] = mean

    first = []
    for d in range(1, ang):
        x_to = lax.rem(a + d, ang)
        eigen_rows(x_to)
        if d == 1:
            await_greetings(ang, pix)
        first.append(send(e_own.at[x_to], e_rows.at[a], s1.at[d], r1.at[d], (x_to, p)))
    eigen_rows(a)
    e_rows[a] = e_own[a]
    for copy in proj_copies:
        copy.wait()
    for copy in first:
        copy.wait_recv()

    def cut_for(q):
        return e_rows.at[q // share, :, pl.ds(pl.multiple_of(lax.rem(q, share) * wide, wide), wide)]

    keep = pltpu.make_async_copy(cut_for(p), e_all.at[a, p], keep_sem)
    keep.start()
    second = []
    for e in range(1, pix):
        q = lax.rem(p + e, pix)
        second.append(send(cut_for(q), e_all.at[a, p], s2.at[e], r2.at[e], (a, q)))
    keep.wait()

    def add_fit(x_at, q):
        for i in range(quarter):
            row = q * rows + x_at * quarter + i
            mean = e_all[x_at, q, quarter * modes + i:quarter * modes + i + 1, :]
            here = strided_row(proj, row, angles, all_rows, range(strips)) - mean
            eigen = e_all[x_at, q, i * modes:(i + 1) * modes, :]
            left = jnp.concatenate(split(here), axis=0)
            right = jnp.concatenate(split(eigen), axis=0)
            fit[...] += dot_nt(left, right)

    third = []
    for e in range(pix):
        q = lax.rem(p + pix - e, pix)
        if e:
            second[e - 1].wait_recv()
        for d in range(1, ang):
            third.append(send(e_all.at[a, q], e_all.at[a, q], s3.at[d, e], r3.at[d, e],
                              (lax.rem(a + d, ang), p)))
        add_fit(a, q)
    for e in range(pix):
        q = lax.rem(p + pix - e, pix)
        for d in range(1, ang):
            third[e * (ang - 1) + d - 1].wait_recv()
            add_fit(lax.rem(a + ang - d, ang), q)
    sums = fit[...]
    part[...] = jnp.zeros_like(part)
    part[:, :modes] = (sums[:angles, :modes] + sums[:angles, modes:]
                       + sums[angles:, :modes] + sums[angles:, modes:])
    fourth = []
    for e in range(1, pix):
        fourth.append(send(part, parts.at[e], s4.at[e], r4.at[e], (a, lax.rem(p + e, pix))))
    whole = part[...]
    for copy in fourth:
        copy.wait_recv()
    for e in range(1, pix):
        whole = whole + parts[e]
    fit_rhs = whole[:, :modes] / npix
    inner = dot_nt(fit_rhs, solver[...], HIGHEST)
    weights = jnp.dot(inner, solver[...], precision=HIGHEST, preferred_element_type=jnp.float32)
    w_high, w_low = split(weights)
    w_all = jnp.concatenate([w_high, w_low, w_high], axis=1)

    def finish(q, carry):
        for x_at in range(ang):
            for i in range(quarter):
                row = q * rows + x_at * quarter + i
                mean = e_all[x_at, q, quarter * modes + i:quarter * modes + i + 1, :]
                e_high, e_low = split(e_all[x_at, q, i * modes:(i + 1) * modes, :])
                e_cat = jnp.concatenate([e_high, e_high, e_low], axis=0)
                estimate = mean + jnp.dot(w_all, e_cat, preferred_element_type=jnp.float32)
                floored = jnp.maximum(estimate, floor_value)
                at = pl.ds(row, angles, stride=all_rows)
                for c in range(strips):
                    done[c, at, :] = proj[c, at, :] / floored[:, c * LANES:(c + 1) * LANES]
        return carry
    lax.fori_loop(0, pix, finish, 0)
    out_copies = []
    for c in range(strips):
        copy = pltpu.make_async_copy(done.at[c], out.at[:, pl.ds(c * LANES, LANES)], out_sem.at[c])
        copy.start()
        out_copies.append(copy)
    for copy in out_copies:
        copy.wait()
    for copy in first + second + third + fourth:
        copy.wait_send()


def correct(flats, projections, basis_t, solver, ang, pix, npix):
    frames, rows, cols = flats.shape
    angles, all_rows, wide = projections.shape
    modes = basis_t.shape[0]
    unit = (rows // ang) * modes + 8
    vmem, dma = pltpu.VMEM, pltpu.SemaphoreType.DMA
    out = pl.pallas_call(
        functools.partial(correct_kernel, ang, pix, frames, rows, angles, all_rows, modes, npix),
        out_shape=jax.ShapeDtypeStruct((angles * all_rows, wide), jnp.float32),
        in_specs=[pl.BlockSpec(memory_space=pl.ANY)] * 2 + [pl.BlockSpec(memory_space=vmem)] * 2,
        out_specs=pl.BlockSpec(memory_space=pl.ANY),
        scratch_shapes=[
            vmem((cols // LANES, frames * rows, LANES), jnp.float32),
            vmem((wide // LANES, angles * all_rows, LANES), jnp.float32),
            vmem((wide // LANES, angles * all_rows, LANES), jnp.float32),
            vmem((ang, unit, cols), jnp.float32),
            vmem((ang, unit, cols), jnp.float32),
            vmem((ang, pix, unit, wide), jnp.float32),
            vmem((2 * angles, 2 * modes), jnp.float32),
            vmem((angles, 128), jnp.float32),
            vmem((pix, angles, 128), jnp.float32),
            dma((cols // LANES,)), dma((wide // LANES,)), dma((wide // LANES,)), dma,
            dma((ang,)), dma((ang,)), dma((pix,)), dma((pix,)),
            dma((ang, pix)), dma((ang, pix)), dma((pix,)), dma((pix,)),
        ],
        compiler_params=pltpu.CompilerParams(
            collective_id=1, has_side_effects=True, vmem_limit_bytes=VMEM_LIMIT
        ),
        name="correct",
    )(flats.reshape(frames * rows, cols), projections.reshape(angles * all_rows, wide),
      basis_t, solver)
    return out.reshape(projections.shape)


def orthonormal(grown):
    correlation = jnp.dot(grown.T, grown, precision=HIGHEST)
    lower = jnp.linalg.cholesky(correlation)
    return jax.scipy.linalg.solve_triangular(lower, grown.T, lower=True).T


def shards(flats, projections, start_basis):
    rows_dev, cols_dev = flats.shape[1:]
    ang, pix = lax.axis_size("ang"), lax.axis_size("pix")
    npix = rows_dev * cols_dev * ang * pix
    gram = gram_of(flats, ang, pix) / npix
    basis = start_basis
    for turn in range(SUBSPACE):
        basis = orthonormal(jnp.dot(gram, basis, precision=HIGHEST))
    normal = jnp.dot(basis.T, jnp.dot(gram, basis, precision=HIGHEST), precision=HIGHEST)
    factor = jnp.linalg.cholesky(normal)
    solver = jax.scipy.linalg.solve_triangular(
        factor, jnp.eye(factor.shape[0], dtype=jnp.float32), lower=True
    )
    return correct(flats, projections, basis.T, solver, ang, pix, npix)


def solution(mesh):
    in_specs = (P(None, "pix", "ang"), P("ang", None, "pix"), P())
    out_specs = P("ang", None, "pix")
    return jax.shard_map(shards, mesh=mesh, in_specs=in_specs, out_specs=out_specs, check_vma=False)
```

```python
import functools

import jax
import jax.numpy as jnp
from jax import lax
from jax.experimental import pallas as pl
from jax.experimental.pallas import tpu as pltpu
from jax.sharding import PartitionSpec as P

SUBSPACE = 2
MESH = pl.DeviceIdType.MESH
HIGHEST = lax.Precision.HIGHEST
VMEM_LIMIT = 56 * 1024 * 1024

floor_value = 0.2


def dot_nt(a, b, precision=None):
    return lax.dot_general(
        a, b, (((1,), (1,)), ((), ())), precision=precision, preferred_element_type=jnp.float32
    )


def split(x):
    high = x.astype(jnp.bfloat16)
    low = (x - high.astype(jnp.float32)).astype(jnp.bfloat16)
    return high, low


def greet(ang, pix, a, p):
    barrier = pltpu.get_barrier_semaphore()
    for d in range(1, ang):
        pl.semaphore_signal(
            barrier, inc=1, device_id=(lax.rem(a + d, ang), p), device_id_type=MESH
        )
    for e in range(1, pix):
        pl.semaphore_signal(
            barrier, inc=1, device_id=(a, lax.rem(p + e, pix)), device_id_type=MESH
        )


def await_greetings(ang, pix):
    pl.semaphore_wait(pltpu.get_barrier_semaphore(), ang + pix - 2)


def send(src, dst, send_sem, recv_sem, device):
    copy = pltpu.make_async_remote_copy(
        src_ref=src, dst_ref=dst, send_sem=send_sem, recv_sem=recv_sem,
        device_id=device, device_id_type=MESH,
    )
    copy.start()
    return copy


LANES = 128


def load_strips(source, target, sems):
    copies = []
    for c in range(target.shape[0]):
        copy = pltpu.make_async_copy(
            source.at[:, pl.ds(c * LANES, LANES)], target.at[c], sems.at[c]
        )
        copy.start()
        copies.append(copy)
    return copies


def strided_row(strips, first, count, stride, group):
    return jnp.concatenate(
        [strips[c, pl.ds(first, count, stride=stride), :] for c in group], axis=1
    )


def gram_kernel(ang, pix, frames, rows, reduce_here, flats, gram, x, acc, cross, total,
                from_ang, from_pix, load_sem, s1, r1, s2, r2, s3, r3, s4, r4):
    a, p = lax.axis_index("ang"), lax.axis_index("pix")
    if reduce_here:
        greet(ang, pix, a, p)
    copies = load_strips(flats, x, load_sem)
    acc[...] = jnp.zeros_like(acc)
    cross[...] = jnp.zeros_like(cross)
    for c in range(0, len(copies), 2):
        copies[c].wait()
        copies[c + 1].wait()

        def one_row(r, carry):
            here = strided_row(x, r, frames, rows, (c, c + 1))
            high, low = split(here - jnp.mean(here, axis=0, keepdims=True))
            acc[...] += dot_nt(high, high)
            cross[...] += dot_nt(high, low)
            return carry
        lax.fori_loop(0, rows, one_row, 0)
    both = cross[...]
    acc[...] += both + both.T
    if not reduce_here:
        gram[...] = acc[...]
        return
    await_greetings(ang, pix)
    block = frames // ang
    piece = block // pix
    first = []
    for d in range(1, ang):
        x_to = lax.rem(a + d, ang)
        first.append(send(acc.at[pl.ds(pl.multiple_of(x_to * block, block), block)],
                          from_ang.at[d], s1.at[d], r1.at[d], (x_to, p)))
    mine = acc[pl.ds(pl.multiple_of(a * block, block), block), :]
    for copy in first:
        copy.wait_recv()
    for d in range(1, ang):
        mine = mine + from_ang[d]
    from_ang[0] = mine
    second = []
    for e in range(1, pix):
        q = lax.rem(p + e, pix)
        second.append(send(from_ang.at[0, pl.ds(pl.multiple_of(q * piece, piece), piece)],
                           from_pix.at[e], s2.at[e], r2.at[e], (a, q)))
    own = from_ang[0, pl.ds(pl.multiple_of(p * piece, piece), piece), :]
    for copy in second:
        copy.wait_recv()
    for e in range(1, pix):
        own = own + from_pix[e]
    at = pl.ds(pl.multiple_of(a * block + p * piece, piece), piece)
    total[at, :] = own
    third = []
    for e in range(1, pix):
        q = lax.rem(p + e, pix)
        third.append(send(total.at[at], total.at[at], s3.at[e], r3.at[e], (a, q)))
    for copy in third:
        copy.wait_recv()
    at = pl.ds(pl.multiple_of(a * block, block), block)
    fourth = []
    for d in range(1, ang):
        x_to = lax.rem(a + d, ang)
        fourth.append(send(total.at[at], total.at[at], s4.at[d], r4.at[d], (x_to, p)))
    for copy in fourth:
        copy.wait_recv()
    gram[...] = total[...]
    for copy in first + second + third + fourth:
        copy.wait_send()


def gram_of(flats, ang, pix):
    frames, rows, cols = flats.shape
    reduce_here = frames % (ang * pix * 8) == 0
    block, piece = frames // ang, max(8, frames // ang // pix)
    vmem, dma = pltpu.VMEM, pltpu.SemaphoreType.DMA
    gram = pl.pallas_call(
        functools.partial(gram_kernel, ang, pix, frames, rows, reduce_here),
        out_shape=jax.ShapeDtypeStruct((frames, frames), jnp.float32),
        in_specs=[pl.BlockSpec(memory_space=pl.ANY)],
        out_specs=pl.BlockSpec(memory_space=vmem),
        scratch_shapes=[
            vmem((cols // LANES, frames * rows, LANES), jnp.float32),
            vmem((frames, frames), jnp.float32),
            vmem((frames, frames), jnp.float32),
            vmem((frames, frames), jnp.float32),
            vmem((ang, block, frames), jnp.float32),
            vmem((pix, piece, frames), jnp.float32),
            dma((cols // LANES,)),
            dma((ang,)), dma((ang,)), dma((pix,)), dma((pix,)),
            dma((pix,)), dma((pix,)), dma((ang,)), dma((ang,)),
        ],
        compiler_params=pltpu.CompilerParams(
            collective_id=0 if reduce_here else None,
            has_side_effects=reduce_here, vmem_limit_bytes=VMEM_LIMIT,
        ),
        name="gram",
    )(flats.reshape(frames * rows, cols))
    return gram if reduce_here else lax.psum(gram, ("ang", "pix"))


def fit_kernel(ang, pix, frames, rows, angles, all_rows, modes, npix,
                   flats, projections, basis_t, solver, eigen_out, weights_out,
                   x, proj, e_own, e_rows, e_all, fit, part, parts,
                   load_sem, proj_sem, store_sem, keep_sem, s1, r1, s2, r2, s3, r3, s4, r4):
    a, p = lax.axis_index("ang"), lax.axis_index("pix")
    greet(ang, pix, a, p)
    copies = load_strips(flats, x, load_sem)
    proj_copies = load_strips(projections, proj, proj_sem)
    quarter = rows // ang
    strips = proj.shape[0]
    wide = strips * LANES
    share = pix // ang
    e_own[...] = jnp.zeros_like(e_own)
    fit[...] = jnp.zeros_like(fit)
    b_high, b_low = split(basis_t[...])
    b_both = jnp.concatenate([b_high, b_low], axis=0)
    for copy in copies:
        copy.wait()

    def eigen_rows(x_to):
        for c in range(0, len(copies), 2):
            cut = pl.ds(c * LANES, 2 * LANES)
            for i in range(quarter):
                here = strided_row(x, x_to * quarter + i, frames, rows, (c, c + 1))
                mean = jnp.mean(here, axis=0, keepdims=True)
                high, low = split(here - mean)
                one = jnp.dot(b_both, high, preferred_element_type=jnp.float32)
                two = jnp.dot(b_high, low, preferred_element_type=jnp.float32)
                e_own[x_to, i * modes:(i + 1) * modes, cut] = one[:modes] + one[modes:] + two
                e_own[x_to, quarter * modes + i:quarter * modes + i + 1, cut] = mean

    first = []
    for d in range(1, ang):
        x_to = lax.rem(a + d, ang)
        eigen_rows(x_to)
        if d == 1:
            await_greetings(ang, pix)
        first.append(send(e_own.at[x_to], e_rows.at[a], s1.at[d], r1.at[d], (x_to, p)))
    eigen_rows(a)
    e_rows[a] = e_own[a]
    for copy in proj_copies:
        copy.wait()
    for copy in first:
        copy.wait_recv()

    def cut_for(q):
        return e_rows.at[q // share, :, pl.ds(pl.multiple_of(lax.rem(q, share) * wide, wide), wide)]

    keep = pltpu.make_async_copy(cut_for(p), e_all.at[a, p], keep_sem)
    keep.start()
    second = []
    for e in range(1, pix):
        q = lax.rem(p + e, pix)
        second.append(send(cut_for(q), e_all.at[a, p], s2.at[e], r2.at[e], (a, q)))
    keep.wait()

    def add_fit(x_at, q):
        for i in range(quarter):
            row = q * rows + x_at * quarter + i
            mean = e_all[x_at, q, quarter * modes + i:quarter * modes + i + 1, :]
            here = strided_row(proj, row, angles, all_rows, range(strips)) - mean
            eigen = e_all[x_at, q, i * modes:(i + 1) * modes, :]
            left = jnp.concatenate(split(here), axis=0)
            right = jnp.concatenate(split(eigen), axis=0)
            fit[...] += dot_nt(left, right)

    across = a + 1 - 2 * lax.rem(a, 2)
    along = lax.rem(a + 2, ang)
    corner = lax.rem(across + 2, ang)
    top = e_all.shape[2] // 16 * 8
    bottom = e_all.shape[2] - top
    to_across, to_along, on_top, on_bottom, stores = [], [], [], [], []

    def pass_on(e, q):
        if e:
            second[e - 1].wait_recv()
        piece = e_all.at[a, q]
        to_across.append(send(piece, piece, s3.at[0, e], r3.at[0, e], (across, p)))
        to_along.append(send(piece, piece, s3.at[1, e], r3.at[1, e], (along, p)))
        add_fit(a, q)

    def forward(e, q):
        to_across[e].wait_recv()
        piece = e_all.at[across, q, pl.ds(0, top)]
        on_top.append(send(piece, piece, s3.at[2, e], r3.at[2, e], (along, p)))
        to_along[e].wait_recv()
        piece = e_all.at[along, q, pl.ds(top, bottom)]
        on_bottom.append(send(piece, piece, s3.at[3, e], r3.at[3, e], (across, p)))
        add_fit(across, q)
        add_fit(along, q)

    def complete(e, q):
        on_top[e].wait_recv()
        on_bottom[e].wait_recv()
        copy = pltpu.make_async_copy(e_all.at[:, q], eigen_out.at[:, q], store_sem.at[e])
        copy.start()
        stores.append(copy)
        add_fit(corner, q)

    for step in range(pix + 2):
        for lag, stage in enumerate((pass_on, forward, complete)):
            e = step - lag
            if 0 <= e < pix:
                stage(e, lax.rem(p + pix - e, pix))
    third = to_across + to_along + on_top + on_bottom
    sums = fit[...]
    part[...] = jnp.zeros_like(part)
    part[:, :modes] = (sums[:angles, :modes] + sums[:angles, modes:]
                       + sums[angles:, :modes] + sums[angles:, modes:])
    fourth = []
    for e in range(1, pix):
        fourth.append(send(part, parts.at[e], s4.at[e], r4.at[e], (a, lax.rem(p + e, pix))))
    whole = part[...]
    for copy in fourth:
        copy.wait_recv()
    for e in range(1, pix):
        whole = whole + parts[e]
    fit_rhs = whole[:, :modes] / npix
    inner = dot_nt(fit_rhs, solver[...], HIGHEST)
    weights = jnp.dot(inner, solver[...], precision=HIGHEST, preferred_element_type=jnp.float32)
    weights_out[...] = jnp.zeros_like(weights_out)
    weights_out[:, :modes] = weights
    for copy in stores:
        copy.wait()
    for copy in first + second + third + fourth:
        copy.wait_send()


def fit_weights(flats, projections, basis_t, solver, ang, pix, npix):
    frames, rows, cols = flats.shape
    angles, all_rows, wide = projections.shape
    modes = basis_t.shape[0]
    unit = (rows // ang) * modes + 8
    vmem, dma = pltpu.VMEM, pltpu.SemaphoreType.DMA
    return pl.pallas_call(
        functools.partial(fit_kernel, ang, pix, frames, rows, angles, all_rows, modes, npix),
        out_shape=(
            jax.ShapeDtypeStruct((ang, pix, unit, wide), jnp.float32),
            jax.ShapeDtypeStruct((angles, LANES), jnp.float32),
        ),
        in_specs=[pl.BlockSpec(memory_space=pl.ANY)] * 2 + [pl.BlockSpec(memory_space=vmem)] * 2,
        out_specs=(pl.BlockSpec(memory_space=pl.ANY), pl.BlockSpec(memory_space=vmem)),
        scratch_shapes=[
            vmem((cols // LANES, frames * rows, LANES), jnp.float32),
            vmem((wide // LANES, angles * all_rows, LANES), jnp.float32),
            vmem((ang, unit, cols), jnp.float32),
            vmem((ang, unit, cols), jnp.float32),
            vmem((ang, pix, unit, wide), jnp.float32),
            vmem((2 * angles, 2 * modes), jnp.float32),
            vmem((angles, LANES), jnp.float32),
            vmem((pix, angles, LANES), jnp.float32),
            dma((cols // LANES,)), dma((wide // LANES,)), dma((pix,)), dma,
            dma((ang,)), dma((ang,)), dma((pix,)), dma((pix,)),
            dma((4, pix)), dma((4, pix)), dma((pix,)), dma((pix,)),
        ],
        compiler_params=pltpu.CompilerParams(
            collective_id=1, has_side_effects=True, vmem_limit_bytes=VMEM_LIMIT
        ),
        name="fit",
    )(flats.reshape(frames * rows, cols), projections.reshape(angles * all_rows, wide),
      basis_t, solver)


def correct_kernel(ang, pix, rows, modes, proj, eigen, weights, out):
    angles = weights.shape[0]
    all_rows = proj.shape[0] // angles
    quarter = rows // ang
    w_high, w_low = split(weights[:, :modes])
    w_all = jnp.concatenate([w_high, w_low, w_high], axis=1)

    def finish(q, carry):
        for x_at in range(ang):
            for i in range(quarter):
                mean = eigen[x_at, q, quarter * modes + i:quarter * modes + i + 1, :]
                e_high, e_low = split(eigen[x_at, q, i * modes:(i + 1) * modes, :])
                e_cat = jnp.concatenate([e_high, e_high, e_low], axis=0)
                estimate = mean + jnp.dot(w_all, e_cat, preferred_element_type=jnp.float32)
                at = pl.ds(q * rows + x_at * quarter + i, angles, stride=all_rows)
                out[at, :] = proj[at, :] / jnp.maximum(estimate, floor_value)
        return carry
    lax.fori_loop(0, pix, finish, 0)


def correct(projections, eigen, weights, rows, modes):
    angles, all_rows, wide = projections.shape
    ang, pix, unit, _ = eigen.shape
    strip = pl.BlockSpec((angles * all_rows, LANES), lambda c: (0, c))
    out = pl.pallas_call(
        functools.partial(correct_kernel, ang, pix, rows, modes),
        grid=(wide // LANES,),
        out_shape=jax.ShapeDtypeStruct((angles * all_rows, wide), jnp.float32),
        in_specs=[
            strip,
            pl.BlockSpec((ang, pix, unit, LANES), lambda c: (0, 0, 0, c)),
            pl.BlockSpec((angles, LANES), lambda c: (0, 0)),
        ],
        out_specs=strip,
        compiler_params=pltpu.CompilerParams(vmem_limit_bytes=VMEM_LIMIT),
        name="correct",
    )(projections.reshape(angles * all_rows, wide), eigen, weights)
    return out.reshape(projections.shape)


def inverse_factor(matrix):
    order = matrix.shape[0]
    side = 64
    place = lax.broadcasted_iota(jnp.int32, (order, order), 0)
    other = lax.broadcasted_iota(jnp.int32, (order, order), 1)
    unit = (place == other).astype(jnp.float32)
    gap = jnp.zeros((order, side - order), jnp.float32)
    table = jnp.concatenate([matrix, gap, unit, gap], axis=1)
    below = lax.broadcasted_iota(jnp.int32, (order, 1), 0)
    for j in range(order - 1):
        row = table[j:j + 1, :]
        factor = table[:, j:j + 1] / table[j:j + 1, j:j + 1]
        table = table - jnp.where(below > j, factor, 0.0) * row
    pivots = jnp.sum(table[:, :order] * unit, axis=1, keepdims=True)
    return table[:, side:side + order] / jnp.sqrt(pivots)


def dot_exact(a, b):
    return jnp.dot(a, b, precision=HIGHEST, preferred_element_type=jnp.float32)


def basis_kernel(npix, gram_ref, start, basis_t, solver):
    gram = gram_ref[...] / npix
    basis = start[...]
    for turn in range(SUBSPACE):
        grown = dot_exact(basis, gram)
        basis = dot_exact(inverse_factor(dot_nt(grown, grown, HIGHEST)), grown)
    basis_t[...] = basis
    normal = dot_nt(dot_exact(basis, gram), basis, HIGHEST)
    solver[...] = inverse_factor(normal)


def basis_of(gram, start_basis, npix):
    modes = start_basis.shape[1]
    return pl.pallas_call(
        functools.partial(basis_kernel, npix),
        out_shape=(
            jax.ShapeDtypeStruct(start_basis.shape[::-1], jnp.float32),
            jax.ShapeDtypeStruct((modes, modes), jnp.float32),
        ),
        compiler_params=pltpu.CompilerParams(vmem_limit_bytes=VMEM_LIMIT),
        name="basis",
    )(gram, start_basis.T)


def shards(flats, projections, start_basis):
    rows_dev, cols_dev = flats.shape[1:]
    ang, pix = lax.axis_size("ang"), lax.axis_size("pix")
    npix = rows_dev * cols_dev * ang * pix
    gram = gram_of(flats, ang, pix)
    basis_t, solver = basis_of(gram, start_basis, npix)
    eigen, weights = fit_weights(flats, projections, basis_t, solver, ang, pix, npix)
    return correct(projections, eigen, weights, rows_dev, basis_t.shape[0])


def solution(mesh):
    in_specs = (P(None, "pix", "ang"), P("ang", None, "pix"), P())
    out_specs = P("ang", None, "pix")
    return jax.shard_map(shards, mesh=mesh, in_specs=in_specs, out_specs=out_specs, check_vma=False)
```

```python
import functools

import jax
import jax.numpy as jnp
from jax import lax
from jax.experimental import pallas as pl
from jax.experimental.pallas import tpu as pltpu
from jax.sharding import PartitionSpec as P

SUBSPACE = 2
MESH = pl.DeviceIdType.MESH
HIGHEST = lax.Precision.HIGHEST
VMEM_LIMIT = 56 * 1024 * 1024

floor_value = 0.2


def dot_nt(a, b, precision=None):
    return lax.dot_general(
        a, b, (((1,), (1,)), ((), ())), precision=precision, preferred_element_type=jnp.float32
    )


def split(x):
    high = x.astype(jnp.bfloat16)
    low = (x - high.astype(jnp.float32)).astype(jnp.bfloat16)
    return high, low


def greet(ang, pix, a, p):
    barrier = pltpu.get_barrier_semaphore()
    for d in range(1, ang):
        pl.semaphore_signal(
            barrier, inc=1, device_id=(lax.rem(a + d, ang), p), device_id_type=MESH
        )
    for e in range(1, pix):
        pl.semaphore_signal(
            barrier, inc=1, device_id=(a, lax.rem(p + e, pix)), device_id_type=MESH
        )


def await_greetings(ang, pix):
    pl.semaphore_wait(pltpu.get_barrier_semaphore(), ang + pix - 2)


def send(src, dst, send_sem, recv_sem, device):
    copy = pltpu.make_async_remote_copy(
        src_ref=src, dst_ref=dst, send_sem=send_sem, recv_sem=recv_sem,
        device_id=device, device_id_type=MESH,
    )
    copy.start()
    return copy


LANES = 128
AHEAD = 4
ROW_GROUP = 4


def load_strips(source, target, sems):
    copies = []
    for c in range(target.shape[0]):
        copy = pltpu.make_async_copy(
            source.at[:, pl.ds(c * LANES, LANES)], target.at[c], sems.at[c]
        )
        copy.start()
        copies.append(copy)
    return copies


def strided_row(strips, first, count, stride, group):
    return jnp.concatenate(
        [strips[c, pl.ds(first, count, stride=stride), :] for c in group], axis=1
    )


def gram_kernel(ang, pix, frames, rows, reduce_here, flats, gram, x, acc, cross, total,
                from_ang, from_pix, load_sem, s1, r1, s2, r2, s3, r3, s4, r4):
    a, p = lax.axis_index("ang"), lax.axis_index("pix")
    if reduce_here:
        greet(ang, pix, a, p)
    copies = load_strips(flats, x, load_sem)
    acc[...] = jnp.zeros_like(acc)
    cross[...] = jnp.zeros_like(cross)
    for c in range(0, len(copies), 2):
        copies[c].wait()
        copies[c + 1].wait()

        def some_rows(turn, carry):
            here = jnp.concatenate(
                [strided_row(x, turn * ROW_GROUP + i, frames, rows, (c, c + 1))
                 for i in range(ROW_GROUP)], axis=1)
            high, low = split(here - jnp.mean(here, axis=0, keepdims=True))
            acc[...] += dot_nt(high, high)
            cross[...] += dot_nt(high, low)
            return carry
        lax.fori_loop(0, rows // ROW_GROUP, some_rows, 0)
    both = cross[...]
    acc[...] += both + both.T
    if not reduce_here:
        gram[...] = acc[...]
        return
    await_greetings(ang, pix)
    block = frames // ang
    piece = block // pix
    first = []
    for d in range(1, ang):
        x_to = lax.rem(a + d, ang)
        first.append(send(acc.at[pl.ds(pl.multiple_of(x_to * block, block), block)],
                          from_ang.at[d], s1.at[d], r1.at[d], (x_to, p)))
    mine = acc[pl.ds(pl.multiple_of(a * block, block), block), :]
    for copy in first:
        copy.wait_recv()
    for d in range(1, ang):
        mine = mine + from_ang[d]
    from_ang[0] = mine
    second = []
    for e in range(1, pix):
        q = lax.rem(p + e, pix)
        second.append(send(from_ang.at[0, pl.ds(pl.multiple_of(q * piece, piece), piece)],
                           from_pix.at[e], s2.at[e], r2.at[e], (a, q)))
    own = from_ang[0, pl.ds(pl.multiple_of(p * piece, piece), piece), :]
    for copy in second:
        copy.wait_recv()
    for e in range(1, pix):
        own = own + from_pix[e]
    at = pl.ds(pl.multiple_of(a * block + p * piece, piece), piece)
    total[at, :] = own
    third = []
    for e in range(1, pix):
        q = lax.rem(p + e, pix)
        third.append(send(total.at[at], total.at[at], s3.at[e], r3.at[e], (a, q)))
    for copy in third:
        copy.wait_recv()
    at = pl.ds(pl.multiple_of(a * block, block), block)
    fourth = []
    for d in range(1, ang):
        x_to = lax.rem(a + d, ang)
        fourth.append(send(total.at[at], total.at[at], s4.at[d], r4.at[d], (x_to, p)))
    for copy in fourth:
        copy.wait_recv()
    gram[...] = total[...]
    for copy in first + second + third + fourth:
        copy.wait_send()


def gram_of(flats, ang, pix):
    frames, rows, cols = flats.shape
    reduce_here = frames % (ang * pix * 8) == 0
    block, piece = frames // ang, max(8, frames // ang // pix)
    vmem, dma = pltpu.VMEM, pltpu.SemaphoreType.DMA
    gram = pl.pallas_call(
        functools.partial(gram_kernel, ang, pix, frames, rows, reduce_here),
        out_shape=jax.ShapeDtypeStruct((frames, frames), jnp.float32),
        in_specs=[pl.BlockSpec(memory_space=pl.ANY)],
        out_specs=pl.BlockSpec(memory_space=vmem),
        scratch_shapes=[
            vmem((cols // LANES, frames * rows, LANES), jnp.float32),
            vmem((frames, frames), jnp.float32),
            vmem((frames, frames), jnp.float32),
            vmem((frames, frames), jnp.float32),
            vmem((ang, block, frames), jnp.float32),
            vmem((pix, piece, frames), jnp.float32),
            dma((cols // LANES,)),
            dma((ang,)), dma((ang,)), dma((pix,)), dma((pix,)),
            dma((pix,)), dma((pix,)), dma((ang,)), dma((ang,)),
        ],
        compiler_params=pltpu.CompilerParams(
            collective_id=0 if reduce_here else None,
            has_side_effects=reduce_here, vmem_limit_bytes=VMEM_LIMIT,
        ),
        name="gram",
    )(flats.reshape(frames * rows, cols))
    return gram if reduce_here else lax.psum(gram, ("ang", "pix"))


def fit_kernel(ang, pix, frames, rows, angles, all_rows, modes, npix,
                   flats, projections, basis_t, solver, eigen_out, weights_out,
                   x, proj, e_own, e_rows, e_all, fit, part, parts,
                   load_sem, proj_sem, store_sem, keep_sem, s1, r1, s2, r2, s3, r3, s4, r4):
    a, p = lax.axis_index("ang"), lax.axis_index("pix")
    greet(ang, pix, a, p)
    copies = load_strips(flats, x, load_sem)
    proj_copies = load_strips(projections, proj, proj_sem)
    quarter = rows // ang
    strips = proj.shape[0]
    wide = strips * LANES
    share = pix // ang
    e_own[...] = jnp.zeros_like(e_own)
    fit[...] = jnp.zeros_like(fit)
    b_high, b_low = split(basis_t[...])
    b_both = jnp.concatenate([b_high, b_low], axis=0)
    for copy in copies:
        copy.wait()

    def eigen_rows(x_to):
        for c in range(0, len(copies), 2):
            cut = pl.ds(c * LANES, 2 * LANES)
            for i in range(quarter):
                here = strided_row(x, x_to * quarter + i, frames, rows, (c, c + 1))
                mean = jnp.mean(here, axis=0, keepdims=True)
                high, low = split(here - mean)
                one = jnp.dot(b_both, high, preferred_element_type=jnp.float32)
                two = jnp.dot(b_high, low, preferred_element_type=jnp.float32)
                e_own[x_to, i * modes:(i + 1) * modes, cut] = one[:modes] + one[modes:] + two
                e_own[x_to, quarter * modes + i:quarter * modes + i + 1, cut] = mean

    first = []
    for d in range(1, ang):
        x_to = lax.rem(a + d, ang)
        eigen_rows(x_to)
        if d == 1:
            await_greetings(ang, pix)
        first.append(send(e_own.at[x_to], e_rows.at[a], s1.at[d], r1.at[d], (x_to, p)))
    eigen_rows(a)
    e_rows[a] = e_own[a]
    for copy in proj_copies:
        copy.wait()
    for copy in first:
        copy.wait_recv()

    def cut_for(q):
        return e_rows.at[q // share, :, pl.ds(pl.multiple_of(lax.rem(q, share) * wide, wide), wide)]

    def partner(e):
        q = p
        for bit in range(pix.bit_length() - 1):
            if (e >> bit) % 2:
                q = q + (1 << bit) * (1 - 2 * lax.rem(p // (1 << bit), 2))
        return q

    def send_columns(e):
        q = partner(e)
        second.append(send(cut_for(q), e_all.at[a, p], s2.at[e], r2.at[e], (a, q)))

    keep = pltpu.make_async_copy(cut_for(p), e_all.at[a, p], keep_sem)
    keep.start()
    second = []
    for e in range(1, AHEAD + 1):
        send_columns(e)
    keep.wait()

    def add_fit(x_at, q):
        for i in range(quarter):
            row = q * rows + x_at * quarter + i
            mean = e_all[x_at, q, quarter * modes + i:quarter * modes + i + 1, :]
            here = strided_row(proj, row, angles, all_rows, range(strips)) - mean
            eigen = e_all[x_at, q, i * modes:(i + 1) * modes, :]
            left = jnp.concatenate(split(here), axis=0)
            right = jnp.concatenate(split(eigen), axis=0)
            fit[...] += dot_nt(left, right)

    across = a + 1 - 2 * lax.rem(a, 2)
    along = lax.rem(a + 2, ang)
    corner = lax.rem(across + 2, ang)
    top = e_all.shape[2] // 16 * 8
    bottom = e_all.shape[2] - top
    to_across, to_along, on_top, on_bottom, stores = [], [], [], [], []

    def pass_on(e, q):
        if e:
            second[e - 1].wait_recv()
            if e + AHEAD < pix:
                send_columns(e + AHEAD)
        piece = e_all.at[a, q]
        to_across.append(send(piece, piece, s3.at[0, e], r3.at[0, e], (across, p)))
        to_along.append(send(piece, piece, s3.at[1, e], r3.at[1, e], (along, p)))
        add_fit(a, q)

    def forward(e, q):
        to_across[e].wait_recv()
        piece = e_all.at[across, q, pl.ds(0, top)]
        on_top.append(send(piece, piece, s3.at[2, e], r3.at[2, e], (along, p)))
        to_along[e].wait_recv()
        piece = e_all.at[along, q, pl.ds(top, bottom)]
        on_bottom.append(send(piece, piece, s3.at[3, e], r3.at[3, e], (across, p)))
        add_fit(across, q)
        add_fit(along, q)

    def complete(e, q):
        on_top[e].wait_recv()
        on_bottom[e].wait_recv()
        copy = pltpu.make_async_copy(e_all.at[:, q], eigen_out.at[:, q], store_sem.at[e])
        copy.start()
        stores.append(copy)
        add_fit(corner, q)

    for step in range(pix + 2):
        for lag, stage in enumerate((pass_on, forward, complete)):
            e = step - lag
            if 0 <= e < pix:
                stage(e, partner(e))
    third = to_across + to_along + on_top + on_bottom
    sums = fit[...]
    part[...] = jnp.zeros_like(part)
    part[:, :modes] = (sums[:angles, :modes] + sums[:angles, modes:]
                       + sums[angles:, :modes] + sums[angles:, modes:])
    fourth = []
    for e in range(1, pix):
        fourth.append(send(part, parts.at[e], s4.at[e], r4.at[e], (a, lax.rem(p + e, pix))))
    whole = part[...]
    for copy in fourth:
        copy.wait_recv()
    for e in range(1, pix):
        whole = whole + parts[e]
    fit_rhs = whole[:, :modes] / npix
    inner = dot_nt(fit_rhs, solver[...], HIGHEST)
    weights = jnp.dot(inner, solver[...], precision=HIGHEST, preferred_element_type=jnp.float32)
    weights_out[...] = jnp.zeros_like(weights_out)
    weights_out[:, :modes] = weights
    for copy in stores:
        copy.wait()
    for copy in first + second + third + fourth:
        copy.wait_send()


def fit_weights(flats, projections, basis_t, solver, ang, pix, npix):
    frames, rows, cols = flats.shape
    angles, all_rows, wide = projections.shape
    modes = basis_t.shape[0]
    unit = (rows // ang) * modes + 8
    vmem, dma = pltpu.VMEM, pltpu.SemaphoreType.DMA
    return pl.pallas_call(
        functools.partial(fit_kernel, ang, pix, frames, rows, angles, all_rows, modes, npix),
        out_shape=(
            jax.ShapeDtypeStruct((ang, pix, unit, wide), jnp.float32),
            jax.ShapeDtypeStruct((angles, LANES), jnp.float32),
        ),
        in_specs=[pl.BlockSpec(memory_space=pl.ANY)] * 2 + [pl.BlockSpec(memory_space=vmem)] * 2,
        out_specs=(pl.BlockSpec(memory_space=pl.ANY), pl.BlockSpec(memory_space=vmem)),
        scratch_shapes=[
            vmem((cols // LANES, frames * rows, LANES), jnp.float32),
            vmem((wide // LANES, angles * all_rows, LANES), jnp.float32),
            vmem((ang, unit, cols), jnp.float32),
            vmem((ang, unit, cols), jnp.float32),
            vmem((ang, pix, unit, wide), jnp.float32),
            vmem((2 * angles, 2 * modes), jnp.float32),
            vmem((angles, LANES), jnp.float32),
            vmem((pix, angles, LANES), jnp.float32),
            dma((cols // LANES,)), dma((wide // LANES,)), dma((pix,)), dma,
            dma((ang,)), dma((ang,)), dma((pix,)), dma((pix,)),
            dma((4, pix)), dma((4, pix)), dma((pix,)), dma((pix,)),
        ],
        compiler_params=pltpu.CompilerParams(
            collective_id=1, has_side_effects=True, vmem_limit_bytes=VMEM_LIMIT
        ),
        name="fit",
    )(flats.reshape(frames * rows, cols), projections.reshape(angles * all_rows, wide),
      basis_t, solver)


def correct_kernel(ang, pix, rows, modes, proj, eigen, weights, out):
    angles = weights.shape[0]
    all_rows = proj.shape[0] // angles
    quarter = rows // ang
    w_high, w_low = split(weights[:, :modes])
    w_all = jnp.concatenate([w_high, w_low, w_high], axis=1)

    def finish(q, carry):
        for x_at in range(ang):
            for i in range(quarter):
                mean = eigen[x_at, q, quarter * modes + i:quarter * modes + i + 1, :]
                e_high, e_low = split(eigen[x_at, q, i * modes:(i + 1) * modes, :])
                e_cat = jnp.concatenate([e_high, e_high, e_low], axis=0)
                estimate = mean + jnp.dot(w_all, e_cat, preferred_element_type=jnp.float32)
                at = pl.ds(q * rows + x_at * quarter + i, angles, stride=all_rows)
                out[at, :] = proj[at, :] / jnp.maximum(estimate, floor_value)
        return carry
    lax.fori_loop(0, pix, finish, 0, unroll=4)


def correct(projections, eigen, weights, rows, modes):
    angles, all_rows, wide = projections.shape
    ang, pix, unit, _ = eigen.shape
    strip = pl.BlockSpec((angles * all_rows, LANES), lambda c: (0, c))
    out = pl.pallas_call(
        functools.partial(correct_kernel, ang, pix, rows, modes),
        grid=(wide // LANES,),
        out_shape=jax.ShapeDtypeStruct((angles * all_rows, wide), jnp.float32),
        in_specs=[
            strip,
            pl.BlockSpec((ang, pix, unit, LANES), lambda c: (0, 0, 0, c)),
            pl.BlockSpec((angles, LANES), lambda c: (0, 0)),
        ],
        out_specs=strip,
        compiler_params=pltpu.CompilerParams(vmem_limit_bytes=VMEM_LIMIT),
        name="correct",
    )(projections.reshape(angles * all_rows, wide), eigen, weights)
    return out.reshape(projections.shape)


def inverse_factor(matrix):
    order = matrix.shape[0]
    side = 64
    place = lax.broadcasted_iota(jnp.int32, (order, order), 0)
    other = lax.broadcasted_iota(jnp.int32, (order, order), 1)
    unit = (place == other).astype(jnp.float32)
    gap = jnp.zeros((order, side - order), jnp.float32)
    table = jnp.concatenate([matrix, gap, unit, gap], axis=1)
    below = lax.broadcasted_iota(jnp.int32, (order, 1), 0)
    for j in range(order - 1):
        row = table[j:j + 1, :]
        factor = table[:, j:j + 1] / table[j:j + 1, j:j + 1]
        table = table - jnp.where(below > j, factor, 0.0) * row
    pivots = jnp.sum(table[:, :order] * unit, axis=1, keepdims=True)
    return table[:, side:side + order] / jnp.sqrt(pivots)


def dot_exact(a, b):
    return jnp.dot(a, b, precision=HIGHEST, preferred_element_type=jnp.float32)


def basis_kernel(npix, gram_ref, start, basis_t, solver):
    gram = gram_ref[...] / npix
    basis = start[...]
    for turn in range(SUBSPACE):
        grown = dot_exact(basis, gram)
        basis = dot_exact(inverse_factor(dot_nt(grown, grown, HIGHEST)), grown)
    basis_t[...] = basis
    normal = dot_nt(dot_exact(basis, gram), basis, HIGHEST)
    solver[...] = inverse_factor(normal)


def basis_of(gram, start_basis, npix):
    modes = start_basis.shape[1]
    return pl.pallas_call(
        functools.partial(basis_kernel, npix),
        out_shape=(
            jax.ShapeDtypeStruct(start_basis.shape[::-1], jnp.float32),
            jax.ShapeDtypeStruct((modes, modes), jnp.float32),
        ),
        compiler_params=pltpu.CompilerParams(vmem_limit_bytes=VMEM_LIMIT),
        name="basis",
    )(gram, start_basis.T)


def shards(flats, projections, start_basis):
    rows_dev, cols_dev = flats.shape[1:]
    ang, pix = lax.axis_size("ang"), lax.axis_size("pix")
    npix = rows_dev * cols_dev * ang * pix
    gram = gram_of(flats, ang, pix)
    basis_t, solver = basis_of(gram, start_basis, npix)
    eigen, weights = fit_weights(flats, projections, basis_t, solver, ang, pix, npix)
    return correct(projections, eigen, weights, rows_dev, basis_t.shape[0])


def solution(mesh):
    in_specs = (P(None, "pix", "ang"), P("ang", None, "pix"), P())
    out_specs = P("ang", None, "pix")
    return jax.shard_map(shards, mesh=mesh, in_specs=in_specs, out_specs=out_specs, check_vma=False)
```

```python
import functools

import jax
import jax.numpy as jnp
from jax import lax
from jax.experimental import pallas as pl
from jax.experimental.pallas import tpu as pltpu
from jax.sharding import PartitionSpec as P

SUBSPACE = 2
MESH = pl.DeviceIdType.MESH
HIGHEST = lax.Precision.HIGHEST
VMEM_LIMIT = 56 * 1024 * 1024

floor_value = 0.2


def dot_nt(a, b, precision=None):
    return lax.dot_general(
        a, b, (((1,), (1,)), ((), ())), precision=precision, preferred_element_type=jnp.float32
    )


def split(x):
    high = x.astype(jnp.bfloat16)
    low = (x - high.astype(jnp.float32)).astype(jnp.bfloat16)
    return high, low


def greet(ang, pix, a, p):
    barrier = pltpu.get_barrier_semaphore()
    for d in range(1, ang):
        pl.semaphore_signal(
            barrier, inc=1, device_id=(lax.rem(a + d, ang), p), device_id_type=MESH
        )
    for e in range(1, pix):
        pl.semaphore_signal(
            barrier, inc=1, device_id=(a, lax.rem(p + e, pix)), device_id_type=MESH
        )


def await_greetings(ang, pix):
    pl.semaphore_wait(pltpu.get_barrier_semaphore(), ang + pix - 2)


def send(src, dst, send_sem, recv_sem, device):
    copy = pltpu.make_async_remote_copy(
        src_ref=src, dst_ref=dst, send_sem=send_sem, recv_sem=recv_sem,
        device_id=device, device_id_type=MESH,
    )
    copy.start()
    return copy


LANES = 128
AHEAD = 4
ROW_GROUP = 4


def load_strips(source, target, sems):
    copies = []
    for c in range(target.shape[0]):
        copy = pltpu.make_async_copy(
            source.at[:, pl.ds(c * LANES, LANES)], target.at[c], sems.at[c]
        )
        copy.start()
        copies.append(copy)
    return copies


def strided_row(strips, first, count, stride, group):
    return jnp.concatenate(
        [strips[c, pl.ds(first, count, stride=stride), :] for c in group], axis=1
    )


def gram_kernel(ang, pix, frames, rows, reduce_here, flats, gram, x, acc, cross, total,
                from_ang, from_pix, load_sem, s1, r1, s2, r2, s3, r3, s4, r4):
    a, p = lax.axis_index("ang"), lax.axis_index("pix")
    if reduce_here:
        greet(ang, pix, a, p)
    copies = load_strips(flats, x, load_sem)
    acc[...] = jnp.zeros_like(acc)
    cross[...] = jnp.zeros_like(cross)
    for c in range(0, len(copies), 2):
        copies[c].wait()
        copies[c + 1].wait()

        def some_rows(turn, carry):
            here = jnp.concatenate(
                [strided_row(x, turn * ROW_GROUP + i, frames, rows, (c, c + 1))
                 for i in range(ROW_GROUP)], axis=1)
            high, low = split(here - jnp.mean(here, axis=0, keepdims=True))
            acc[...] += dot_nt(high, high)
            cross[...] += dot_nt(high, low)
            return carry
        lax.fori_loop(0, rows // ROW_GROUP, some_rows, 0)
    both = cross[...]
    acc[...] += both + both.T
    if not reduce_here:
        gram[...] = acc[...]
        return
    await_greetings(ang, pix)
    block = frames // ang
    piece = block // pix
    first = []
    for d in range(1, ang):
        x_to = lax.rem(a + d, ang)
        first.append(send(acc.at[pl.ds(pl.multiple_of(x_to * block, block), block)],
                          from_ang.at[d], s1.at[d], r1.at[d], (x_to, p)))
    mine = acc[pl.ds(pl.multiple_of(a * block, block), block), :]
    for copy in first:
        copy.wait_recv()
    for d in range(1, ang):
        mine = mine + from_ang[d]
    from_ang[0] = mine
    second = []
    for e in range(1, pix):
        q = lax.rem(p + e, pix)
        second.append(send(from_ang.at[0, pl.ds(pl.multiple_of(q * piece, piece), piece)],
                           from_pix.at[e], s2.at[e], r2.at[e], (a, q)))
    own = from_ang[0, pl.ds(pl.multiple_of(p * piece, piece), piece), :]
    for copy in second:
        copy.wait_recv()
    for e in range(1, pix):
        own = own + from_pix[e]
    at = pl.ds(pl.multiple_of(a * block + p * piece, piece), piece)
    total[at, :] = own
    third = []
    for e in range(1, pix):
        q = lax.rem(p + e, pix)
        third.append(send(total.at[at], total.at[at], s3.at[e], r3.at[e], (a, q)))
    for copy in third:
        copy.wait_recv()
    at = pl.ds(pl.multiple_of(a * block, block), block)
    fourth = []
    for d in range(1, ang):
        x_to = lax.rem(a + d, ang)
        fourth.append(send(total.at[at], total.at[at], s4.at[d], r4.at[d], (x_to, p)))
    for copy in fourth:
        copy.wait_recv()
    gram[...] = total[...]
    for copy in first + second + third + fourth:
        copy.wait_send()


def gram_of(flats, ang, pix):
    frames, rows, cols = flats.shape
    reduce_here = frames % (ang * pix * 8) == 0
    block, piece = frames // ang, max(8, frames // ang // pix)
    vmem, dma = pltpu.VMEM, pltpu.SemaphoreType.DMA
    gram = pl.pallas_call(
        functools.partial(gram_kernel, ang, pix, frames, rows, reduce_here),
        out_shape=jax.ShapeDtypeStruct((frames, frames), jnp.float32),
        in_specs=[pl.BlockSpec(memory_space=pl.ANY)],
        out_specs=pl.BlockSpec(memory_space=vmem),
        scratch_shapes=[
            vmem((cols // LANES, frames * rows, LANES), jnp.float32),
            vmem((frames, frames), jnp.float32),
            vmem((frames, frames), jnp.float32),
            vmem((frames, frames), jnp.float32),
            vmem((ang, block, frames), jnp.float32),
            vmem((pix, piece, frames), jnp.float32),
            dma((cols // LANES,)),
            dma((ang,)), dma((ang,)), dma((pix,)), dma((pix,)),
            dma((pix,)), dma((pix,)), dma((ang,)), dma((ang,)),
        ],
        compiler_params=pltpu.CompilerParams(
            collective_id=0 if reduce_here else None,
            has_side_effects=reduce_here, vmem_limit_bytes=VMEM_LIMIT,
        ),
        name="gram",
    )(flats.reshape(frames * rows, cols))
    return gram if reduce_here else lax.psum(gram, ("ang", "pix"))


def fit_kernel(ang, pix, frames, rows, angles, all_rows, modes, npix,
                   flats, projections, gram_ref, start, eigen_out, weights_out,
                   x, proj, solver, e_own, e_rows, e_all, fit, part, parts,
                   load_sem, proj_sem, store_sem, keep_sem, s1, r1, s2, r2, s3, r3, s4, r4):
    a, p = lax.axis_index("ang"), lax.axis_index("pix")
    greet(ang, pix, a, p)
    copies = load_strips(flats, x, load_sem)
    proj_copies = load_strips(projections, proj, proj_sem)
    quarter = rows // ang
    strips = proj.shape[0]
    wide = strips * LANES
    share = pix // ang
    e_own[...] = jnp.zeros_like(e_own)
    fit[...] = jnp.zeros_like(fit)
    gram = gram_ref[...] / npix
    basis_t = start[...]
    for turn in range(SUBSPACE):
        grown = dot_exact(basis_t, gram)
        basis_t = dot_exact(inverse_factor(dot_nt(grown, grown, HIGHEST)), grown)
    b_high, b_low = split(basis_t)
    b_both = jnp.concatenate([b_high, b_low], axis=0)
    for copy in copies:
        copy.wait()

    def eigen_rows(x_to):
        for c in range(0, len(copies), 2):
            cut = pl.ds(c * LANES, 2 * LANES)
            for i in range(quarter):
                here = strided_row(x, x_to * quarter + i, frames, rows, (c, c + 1))
                mean = jnp.mean(here, axis=0, keepdims=True)
                high, low = split(here - mean)
                one = jnp.dot(b_both, high, preferred_element_type=jnp.float32)
                two = jnp.dot(b_high, low, preferred_element_type=jnp.float32)
                e_own[x_to, i * modes:(i + 1) * modes, cut] = one[:modes] + one[modes:] + two
                e_own[x_to, quarter * modes + i:quarter * modes + i + 1, cut] = mean

    first = []
    for d in range(1, ang):
        x_to = lax.rem(a + d, ang)
        eigen_rows(x_to)
        if d == 1:
            await_greetings(ang, pix)
        first.append(send(e_own.at[x_to], e_rows.at[a], s1.at[d], r1.at[d], (x_to, p)))
    eigen_rows(a)
    e_rows[a] = e_own[a]
    normal = dot_nt(dot_exact(basis_t, gram), basis_t, HIGHEST)
    solver[...] = inverse_factor(normal)
    for copy in proj_copies:
        copy.wait()
    for copy in first:
        copy.wait_recv()

    def cut_for(q):
        return e_rows.at[q // share, :, pl.ds(pl.multiple_of(lax.rem(q, share) * wide, wide), wide)]

    def partner(e):
        q = p
        for bit in range(pix.bit_length() - 1):
            if (e >> bit) % 2:
                q = q + (1 << bit) * (1 - 2 * lax.rem(p // (1 << bit), 2))
        return q

    def send_columns(e):
        q = partner(e)
        second.append(send(cut_for(q), e_all.at[a, p], s2.at[e], r2.at[e], (a, q)))

    keep = pltpu.make_async_copy(cut_for(p), e_all.at[a, p], keep_sem)
    keep.start()
    second = []
    for e in range(1, AHEAD + 1):
        send_columns(e)
    keep.wait()

    def add_fit(x_at, q):
        for i in range(quarter):
            row = q * rows + x_at * quarter + i
            mean = e_all[x_at, q, quarter * modes + i:quarter * modes + i + 1, :]
            here = strided_row(proj, row, angles, all_rows, range(strips)) - mean
            eigen = e_all[x_at, q, i * modes:(i + 1) * modes, :]
            left = jnp.concatenate(split(here), axis=0)
            right = jnp.concatenate(split(eigen), axis=0)
            fit[...] += dot_nt(left, right)

    across = a + 1 - 2 * lax.rem(a, 2)
    along = lax.rem(a + 2, ang)
    corner = lax.rem(across + 2, ang)
    top = e_all.shape[2] // 16 * 8
    bottom = e_all.shape[2] - top
    to_across, to_along, on_top, on_bottom, stores = [], [], [], [], []

    def pass_on(e, q):
        if e:
            second[e - 1].wait_recv()
            if e + AHEAD < pix:
                send_columns(e + AHEAD)
        piece = e_all.at[a, q]
        to_across.append(send(piece, piece, s3.at[0, e], r3.at[0, e], (across, p)))
        to_along.append(send(piece, piece, s3.at[1, e], r3.at[1, e], (along, p)))
        add_fit(a, q)

    def forward(e, q):
        to_across[e].wait_recv()
        piece = e_all.at[across, q, pl.ds(0, top)]
        on_top.append(send(piece, piece, s3.at[2, e], r3.at[2, e], (along, p)))
        to_along[e].wait_recv()
        piece = e_all.at[along, q, pl.ds(top, bottom)]
        on_bottom.append(send(piece, piece, s3.at[3, e], r3.at[3, e], (across, p)))
        add_fit(across, q)
        add_fit(along, q)

    def complete(e, q):
        on_top[e].wait_recv()
        on_bottom[e].wait_recv()
        copy = pltpu.make_async_copy(e_all.at[:, q], eigen_out.at[:, q], store_sem.at[e])
        copy.start()
        stores.append(copy)
        add_fit(corner, q)

    for step in range(pix + 2):
        for lag, stage in enumerate((pass_on, forward, complete)):
            e = step - lag
            if 0 <= e < pix:
                stage(e, partner(e))
    third = to_across + to_along + on_top + on_bottom
    sums = fit[...]
    part[...] = jnp.zeros_like(part)
    part[:, :modes] = (sums[:angles, :modes] + sums[:angles, modes:]
                       + sums[angles:, :modes] + sums[angles:, modes:])
    fourth = []
    for e in range(1, pix):
        fourth.append(send(part, parts.at[e], s4.at[e], r4.at[e], (a, lax.rem(p + e, pix))))
    whole = part[...]
    for copy in fourth:
        copy.wait_recv()
    for e in range(1, pix):
        whole = whole + parts[e]
    fit_rhs = whole[:, :modes] / npix
    inner = dot_nt(fit_rhs, solver[...], HIGHEST)
    weights = jnp.dot(inner, solver[...], precision=HIGHEST, preferred_element_type=jnp.float32)
    weights_out[...] = jnp.ones_like(weights_out)
    weights_out[:, :modes] = weights
    for copy in stores:
        copy.wait()
    for copy in first + second + third + fourth:
        copy.wait_send()


def fit_weights(flats, projections, gram, start_basis, ang, pix, npix):
    frames, rows, cols = flats.shape
    angles, all_rows, wide = projections.shape
    modes = start_basis.shape[1]
    unit = (rows // ang) * modes + 8
    vmem, dma = pltpu.VMEM, pltpu.SemaphoreType.DMA
    return pl.pallas_call(
        functools.partial(fit_kernel, ang, pix, frames, rows, angles, all_rows, modes, npix),
        out_shape=(
            jax.ShapeDtypeStruct((ang, pix, unit, wide), jnp.float32),
            jax.ShapeDtypeStruct((angles, LANES), jnp.float32),
        ),
        in_specs=[pl.BlockSpec(memory_space=pl.ANY)] * 2 + [pl.BlockSpec(memory_space=vmem)] * 2,
        out_specs=(pl.BlockSpec(memory_space=pl.ANY), pl.BlockSpec(memory_space=vmem)),
        scratch_shapes=[
            vmem((cols // LANES, frames * rows, LANES), jnp.float32),
            vmem((wide // LANES, angles * all_rows, LANES), jnp.float32),
            vmem((modes, modes), jnp.float32),
            vmem((ang, unit, cols), jnp.float32),
            vmem((ang, unit, cols), jnp.float32),
            vmem((ang, pix, unit, wide), jnp.float32),
            vmem((2 * angles, 2 * modes), jnp.float32),
            vmem((angles, LANES), jnp.float32),
            vmem((pix, angles, LANES), jnp.float32),
            dma((cols // LANES,)), dma((wide // LANES,)), dma((pix,)), dma,
            dma((ang,)), dma((ang,)), dma((pix,)), dma((pix,)),
            dma((4, pix)), dma((4, pix)), dma((pix,)), dma((pix,)),
        ],
        compiler_params=pltpu.CompilerParams(
            collective_id=1, has_side_effects=True, vmem_limit_bytes=VMEM_LIMIT
        ),
        name="fit",
    )(flats.reshape(frames * rows, cols), projections.reshape(angles * all_rows, wide),
      gram, start_basis.T)


def correct_kernel(rows, modes, proj, eigen, weights, out, spread_high, spread_low):
    angles = weights.shape[0]
    ang, _, unit, wide = eigen.shape
    quarter = rows // ang
    tall, depth = angles * rows, ang * unit

    @pl.when(pl.program_id(0) == 0)
    def _():
        column = lax.broadcasted_iota(jnp.int32, (LANES, depth), 1)
        within = lax.rem(column, unit)
        is_mean = within >= quarter * modes
        source = jnp.where(is_mean, modes, lax.rem(within, modes))
        pick = (source == lax.broadcasted_iota(jnp.int32, (LANES, depth), 0)).astype(jnp.bfloat16)
        column = lax.broadcasted_iota(jnp.int32, (tall, depth), 1)
        within = lax.rem(column, unit)
        place = jnp.where(within >= quarter * modes, within - quarter * modes, within // modes)
        row = lax.rem(lax.broadcasted_iota(jnp.int32, (tall, depth), 0), rows)
        own = (place < quarter) & (column // unit * quarter + place == row)
        every = jnp.broadcast_to(weights[...][:, None, :], (angles, rows, LANES))
        for part, spread in zip(split(every.reshape(tall, LANES)), (spread_high, spread_low)):
            laid = jnp.dot(part, pick, preferred_element_type=jnp.float32)
            spread[...] = jnp.where(own, laid, 0.0).astype(jnp.bfloat16)

    e_high, e_low = split(eigen[...].reshape(depth, wide))
    estimate = jnp.dot(spread_high[...], e_high, preferred_element_type=jnp.float32)
    estimate += jnp.dot(spread_low[...], e_high, preferred_element_type=jnp.float32)
    estimate += jnp.dot(spread_high[...], e_low, preferred_element_type=jnp.float32)
    floored = jnp.maximum(estimate, floor_value)
    out[...] = proj[...] / floored.reshape(angles, rows, wide)


def correct(projections, eigen, weights, rows, modes):
    angles, _, wide = projections.shape
    ang, pix, unit, _ = eigen.shape
    frame = pl.BlockSpec((angles, rows, wide), lambda q: (0, q, 0))
    return pl.pallas_call(
        functools.partial(correct_kernel, rows, modes),
        grid=(pix,),
        out_shape=jax.ShapeDtypeStruct(projections.shape, jnp.float32),
        in_specs=[
            frame,
            pl.BlockSpec((ang, 1, unit, wide), lambda q: (0, q, 0, 0)),
            pl.BlockSpec((angles, LANES), lambda q: (0, 0)),
        ],
        out_specs=frame,
        scratch_shapes=[pltpu.VMEM((angles * rows, ang * unit), jnp.bfloat16)] * 2,
        compiler_params=pltpu.CompilerParams(vmem_limit_bytes=VMEM_LIMIT),
        name="correct",
    )(projections, eigen, weights)


def inverse_factor(matrix):
    order = matrix.shape[0]
    side = 64
    place = lax.broadcasted_iota(jnp.int32, (order, order), 0)
    other = lax.broadcasted_iota(jnp.int32, (order, order), 1)
    unit = (place == other).astype(jnp.float32)
    gap = jnp.zeros((order, side - order), jnp.float32)
    table = jnp.concatenate([matrix, gap, unit, gap], axis=1)
    below = lax.broadcasted_iota(jnp.int32, (order, 1), 0)
    for j in range(order - 1):
        row = table[j:j + 1, :]
        factor = table[:, j:j + 1] / table[j:j + 1, j:j + 1]
        table = table - jnp.where(below > j, factor, 0.0) * row
    pivots = jnp.sum(table[:, :order] * unit, axis=1, keepdims=True)
    return table[:, side:side + order] / jnp.sqrt(pivots)


def dot_exact(a, b):
    return jnp.dot(a, b, precision=HIGHEST, preferred_element_type=jnp.float32)


def shards(flats, projections, start_basis):
    rows_dev, cols_dev = flats.shape[1:]
    ang, pix = lax.axis_size("ang"), lax.axis_size("pix")
    npix = rows_dev * cols_dev * ang * pix
    gram = gram_of(flats, ang, pix)
    eigen, weights = fit_weights(flats, projections, gram, start_basis, ang, pix, npix)
    return correct(projections, eigen, weights, rows_dev, start_basis.shape[1])


def solution(mesh):
    in_specs = (P(None, "pix", "ang"), P("ang", None, "pix"), P())
    out_specs = P("ang", None, "pix")
    return jax.shard_map(shards, mesh=mesh, in_specs=in_specs, out_specs=out_specs, check_vma=False)
```

```python
import functools

import jax
import jax.numpy as jnp
from jax import lax
from jax.experimental import pallas as pl
from jax.experimental.pallas import tpu as pltpu
from jax.sharding import PartitionSpec as P

SUBSPACE = 2
MESH = pl.DeviceIdType.MESH
HIGHEST = lax.Precision.HIGHEST
VMEM_LIMIT = 56 * 1024 * 1024

floor_value = 0.2


def dot_nt(a, b, precision=None):
    return lax.dot_general(
        a, b, (((1,), (1,)), ((), ())), precision=precision, preferred_element_type=jnp.float32
    )


def split(x):
    high = x.astype(jnp.bfloat16)
    low = (x - high.astype(jnp.float32)).astype(jnp.bfloat16)
    return high, low


def greet(ang, pix, a, p):
    barrier = pltpu.get_barrier_semaphore()
    for d in range(1, ang):
        pl.semaphore_signal(
            barrier, inc=1, device_id=(lax.rem(a + d, ang), p), device_id_type=MESH
        )
    for e in range(1, pix):
        pl.semaphore_signal(
            barrier, inc=1, device_id=(a, lax.rem(p + e, pix)), device_id_type=MESH
        )


def await_greetings(ang, pix):
    pl.semaphore_wait(pltpu.get_barrier_semaphore(), ang + pix - 2)


def send(src, dst, send_sem, recv_sem, device):
    copy = pltpu.make_async_remote_copy(
        src_ref=src, dst_ref=dst, send_sem=send_sem, recv_sem=recv_sem,
        device_id=device, device_id_type=MESH,
    )
    copy.start()
    return copy


LANES = 128
AHEAD = 4
ROW_GROUP = 4


def load_strips(source, target, sems):
    copies = []
    for c in range(target.shape[0]):
        copy = pltpu.make_async_copy(
            source.at[:, pl.ds(c * LANES, LANES)], target.at[c], sems.at[c]
        )
        copy.start()
        copies.append(copy)
    return copies


def strided_row(strips, first, count, stride, group):
    return jnp.concatenate(
        [strips[c, pl.ds(first, count, stride=stride), :] for c in group], axis=1
    )


def gram_kernel(ang, pix, frames, rows, reduce_here, flats, gram, x, acc, cross, total,
                from_ang, from_pix, load_sem, s1, r1, s2, r2, s3, r3, s4, r4):
    a, p = lax.axis_index("ang"), lax.axis_index("pix")
    if reduce_here:
        greet(ang, pix, a, p)
    copies = load_strips(flats, x, load_sem)
    acc[...] = jnp.zeros_like(acc)
    cross[...] = jnp.zeros_like(cross)
    for c in range(0, len(copies), 2):
        copies[c].wait()
        copies[c + 1].wait()

        def some_rows(turn, carry):
            here = jnp.concatenate(
                [strided_row(x, turn * ROW_GROUP + i, frames, rows, (c, c + 1))
                 for i in range(ROW_GROUP)], axis=1)
            high, low = split(here - jnp.mean(here, axis=0, keepdims=True))
            acc[...] += dot_nt(high, high)
            cross[...] += dot_nt(high, low)
            return carry
        lax.fori_loop(0, rows // ROW_GROUP, some_rows, 0)
    both = cross[...]
    acc[...] += both + both.T
    if not reduce_here:
        gram[...] = acc[...]
        return
    await_greetings(ang, pix)
    block = frames // ang
    piece = block // pix
    first = []
    for d in range(1, ang):
        x_to = lax.rem(a + d, ang)
        first.append(send(acc.at[pl.ds(pl.multiple_of(x_to * block, block), block)],
                          from_ang.at[d], s1.at[d], r1.at[d], (x_to, p)))
    mine = acc[pl.ds(pl.multiple_of(a * block, block), block), :]
    for copy in first:
        copy.wait_recv()
    for d in range(1, ang):
        mine = mine + from_ang[d]
    from_ang[0] = mine
    second = []
    for e in range(1, pix):
        q = lax.rem(p + e, pix)
        second.append(send(from_ang.at[0, pl.ds(pl.multiple_of(q * piece, piece), piece)],
                           from_pix.at[e], s2.at[e], r2.at[e], (a, q)))
    own = from_ang[0, pl.ds(pl.multiple_of(p * piece, piece), piece), :]
    for copy in second:
        copy.wait_recv()
    for e in range(1, pix):
        own = own + from_pix[e]
    at = pl.ds(pl.multiple_of(a * block + p * piece, piece), piece)
    total[at, :] = own
    third = []
    for e in range(1, pix):
        q = lax.rem(p + e, pix)
        third.append(send(total.at[at], total.at[at], s3.at[e], r3.at[e], (a, q)))
    for copy in third:
        copy.wait_recv()
    at = pl.ds(pl.multiple_of(a * block, block), block)
    fourth = []
    for d in range(1, ang):
        x_to = lax.rem(a + d, ang)
        fourth.append(send(total.at[at], total.at[at], s4.at[d], r4.at[d], (x_to, p)))
    for copy in fourth:
        copy.wait_recv()
    gram[...] = total[...]
    for copy in first + second + third + fourth:
        copy.wait_send()


def gram_of(flats, ang, pix):
    frames, rows, cols = flats.shape
    reduce_here = frames % (ang * pix * 8) == 0
    block, piece = frames // ang, max(8, frames // ang // pix)
    vmem, dma = pltpu.VMEM, pltpu.SemaphoreType.DMA
    gram = pl.pallas_call(
        functools.partial(gram_kernel, ang, pix, frames, rows, reduce_here),
        out_shape=jax.ShapeDtypeStruct((frames, frames), jnp.float32),
        in_specs=[pl.BlockSpec(memory_space=pl.ANY)],
        out_specs=pl.BlockSpec(memory_space=vmem),
        scratch_shapes=[
            vmem((cols // LANES, frames * rows, LANES), jnp.float32),
            vmem((frames, frames), jnp.float32),
            vmem((frames, frames), jnp.float32),
            vmem((frames, frames), jnp.float32),
            vmem((ang, block, frames), jnp.float32),
            vmem((pix, piece, frames), jnp.float32),
            dma((cols // LANES,)),
            dma((ang,)), dma((ang,)), dma((pix,)), dma((pix,)),
            dma((pix,)), dma((pix,)), dma((ang,)), dma((ang,)),
        ],
        compiler_params=pltpu.CompilerParams(
            collective_id=0 if reduce_here else None,
            has_side_effects=reduce_here, vmem_limit_bytes=VMEM_LIMIT,
        ),
        name="gram",
    )(flats.reshape(frames * rows, cols))
    return gram if reduce_here else lax.psum(gram, ("ang", "pix"))


def fit_kernel(ang, pix, frames, rows, angles, all_rows, modes, npix,
                   flats, projections, gram_ref, start, eigen_out, weights_out,
                   x, proj, solver, e_own, e_rows, e_all, fit, part, parts,
                   load_sem, proj_sem, store_sem, keep_sem, s1, r1, s2, r2, s3, r3, s4, r4):
    a, p = lax.axis_index("ang"), lax.axis_index("pix")
    greet(ang, pix, a, p)
    copies = load_strips(flats, x, load_sem)
    proj_copies = load_strips(projections, proj, proj_sem)
    quarter = rows // ang
    strips = proj.shape[0]
    wide = strips * LANES
    share = pix // ang
    e_own[...] = jnp.zeros_like(e_own)
    fit[...] = jnp.zeros_like(fit)
    gram = gram_ref[...] / npix
    basis_t = start[...]
    for turn in range(SUBSPACE):
        grown = dot_exact(basis_t, gram)
        basis_t = dot_exact(inverse_factor(dot_nt(grown, grown, HIGHEST)), grown)
    b_high, b_low = split(basis_t)
    b_both = jnp.concatenate([b_high, b_low], axis=0)
    for copy in copies:
        copy.wait()

    def eigen_rows(x_to):
        for c in range(0, len(copies), 2):
            cut = pl.ds(c * LANES, 2 * LANES)
            for i in range(quarter):
                here = strided_row(x, x_to * quarter + i, frames, rows, (c, c + 1))
                mean = jnp.mean(here, axis=0, keepdims=True)
                high, low = split(here - mean)
                one = jnp.dot(b_both, high, preferred_element_type=jnp.float32)
                two = jnp.dot(b_high, low, preferred_element_type=jnp.float32)
                e_own[x_to, i * modes:(i + 1) * modes, cut] = one[:modes] + one[modes:] + two
                e_own[x_to, quarter * modes + i:quarter * modes + i + 1, cut] = mean

    first = []
    for d in range(1, ang):
        x_to = lax.rem(a + d, ang)
        eigen_rows(x_to)
        if d == 1:
            await_greetings(ang, pix)
        first.append(send(e_own.at[x_to], e_rows.at[a], s1.at[d], r1.at[d], (x_to, p)))
    eigen_rows(a)
    e_rows[a] = e_own[a]
    normal = dot_nt(dot_exact(basis_t, gram), basis_t, HIGHEST)
    solver[...] = inverse_factor(normal)
    for copy in proj_copies:
        copy.wait()
    for copy in first:
        copy.wait_recv()

    def cut_for(q):
        return e_rows.at[q // share, :, pl.ds(pl.multiple_of(lax.rem(q, share) * wide, wide), wide)]

    def partner(e):
        q = p
        for bit in range(pix.bit_length() - 1):
            if (e >> bit) % 2:
                q = q + (1 << bit) * (1 - 2 * lax.rem(p // (1 << bit), 2))
        return q

    def send_columns(e):
        q = partner(e)
        second.append(send(cut_for(q), e_all.at[a, p], s2.at[e], r2.at[e], (a, q)))

    keep = pltpu.make_async_copy(cut_for(p), e_all.at[a, p], keep_sem)
    keep.start()
    second = []
    for e in range(1, AHEAD + 1):
        send_columns(e)
    keep.wait()

    def add_fit(x_at, q):
        for i in range(quarter):
            row = q * rows + x_at * quarter + i
            mean = e_all[x_at, q, quarter * modes + i:quarter * modes + i + 1, :]
            here = strided_row(proj, row, angles, all_rows, range(strips)) - mean
            eigen = e_all[x_at, q, i * modes:(i + 1) * modes, :]
            left = jnp.concatenate(split(here), axis=0)
            right = jnp.concatenate(split(eigen), axis=0)
            fit[...] += dot_nt(left, right)

    across = a + 1 - 2 * lax.rem(a, 2)
    along = lax.rem(a + 2, ang)
    corner = lax.rem(across + 2, ang)
    top = e_all.shape[2] // 16 * 8
    bottom = e_all.shape[2] - top
    to_across, to_along, on_top, on_bottom, stores = [], [], [], [], []

    def pass_on(e, q):
        if e:
            second[e - 1].wait_recv()
            if e + AHEAD < pix:
                send_columns(e + AHEAD)
        piece = e_all.at[a, q]
        to_across.append(send(piece, piece, s3.at[0, e], r3.at[0, e], (across, p)))
        to_along.append(send(piece, piece, s3.at[1, e], r3.at[1, e], (along, p)))
        add_fit(a, q)

    def forward(e, q):
        to_across[e].wait_recv()
        piece = e_all.at[across, q, pl.ds(0, top)]
        on_top.append(send(piece, piece, s3.at[2, e], r3.at[2, e], (along, p)))
        to_along[e].wait_recv()
        piece = e_all.at[along, q, pl.ds(top, bottom)]
        on_bottom.append(send(piece, piece, s3.at[3, e], r3.at[3, e], (across, p)))
        add_fit(across, q)
        add_fit(along, q)

    def complete(e, q):
        on_top[e].wait_recv()
        on_bottom[e].wait_recv()
        copy = pltpu.make_async_copy(e_all.at[:, q], eigen_out.at[:, q], store_sem.at[e])
        copy.start()
        stores.append(copy)
        add_fit(corner, q)

    for step in range(pix + 2):
        for lag, stage in enumerate((pass_on, forward, complete)):
            e = step - lag
            if 0 <= e < pix:
                stage(e, partner(e))
    third = to_across + to_along + on_top + on_bottom
    sums = fit[...]
    part[...] = jnp.zeros_like(part)
    part[:, :modes] = (sums[:angles, :modes] + sums[:angles, modes:]
                       + sums[angles:, :modes] + sums[angles:, modes:])
    fourth = []
    for e in range(1, pix):
        fourth.append(send(part, parts.at[e], s4.at[e], r4.at[e], (a, lax.rem(p + e, pix))))
    whole = part[...]
    for copy in fourth:
        copy.wait_recv()
    for e in range(1, pix):
        whole = whole + parts[e]
    fit_rhs = whole[:, :modes] / npix
    inner = dot_nt(fit_rhs, solver[...], HIGHEST)
    weights = jnp.dot(inner, solver[...], precision=HIGHEST, preferred_element_type=jnp.float32)
    weights_out[...] = jnp.ones_like(weights_out)
    weights_out[:, :modes] = weights
    for copy in stores:
        copy.wait()
    for copy in first + second + third + fourth:
        copy.wait_send()


def fit_weights(flats, projections, gram, start_basis, ang, pix, npix):
    frames, rows, cols = flats.shape
    angles, all_rows, wide = projections.shape
    modes = start_basis.shape[1]
    unit = (rows // ang) * modes + 8
    vmem, dma = pltpu.VMEM, pltpu.SemaphoreType.DMA
    return pl.pallas_call(
        functools.partial(fit_kernel, ang, pix, frames, rows, angles, all_rows, modes, npix),
        out_shape=(
            jax.ShapeDtypeStruct((ang, pix, unit, wide), jnp.float32),
            jax.ShapeDtypeStruct((angles, LANES), jnp.float32),
        ),
        in_specs=[pl.BlockSpec(memory_space=pl.ANY)] * 2 + [pl.BlockSpec(memory_space=vmem)] * 2,
        out_specs=(pl.BlockSpec(memory_space=pl.ANY), pl.BlockSpec(memory_space=vmem)),
        scratch_shapes=[
            vmem((cols // LANES, frames * rows, LANES), jnp.float32),
            vmem((wide // LANES, angles * all_rows, LANES), jnp.float32),
            vmem((modes, modes), jnp.float32),
            vmem((ang, unit, cols), jnp.float32),
            vmem((ang, unit, cols), jnp.float32),
            vmem((ang, pix, unit, wide), jnp.float32),
            vmem((2 * angles, 2 * modes), jnp.float32),
            vmem((angles, LANES), jnp.float32),
            vmem((pix, angles, LANES), jnp.float32),
            dma((cols // LANES,)), dma((wide // LANES,)), dma((pix,)), dma,
            dma((ang,)), dma((ang,)), dma((pix,)), dma((pix,)),
            dma((4, pix)), dma((4, pix)), dma((pix,)), dma((pix,)),
        ],
        compiler_params=pltpu.CompilerParams(
            collective_id=1, has_side_effects=True, vmem_limit_bytes=VMEM_LIMIT
        ),
        name="fit",
    )(flats.reshape(frames * rows, cols), projections.reshape(angles * all_rows, wide),
      gram, start_basis.T)


def correct_kernel(rows, modes, proj, eigen, weights, out, spread_high, spread_low):
    angles = weights.shape[0]
    ang, _, unit, wide = eigen.shape
    quarter = rows // ang
    tall, depth = angles * rows, ang * unit

    @pl.when(pl.program_id(0) == 0)
    def _():
        column = lax.broadcasted_iota(jnp.int32, (1, depth), 1)
        within = lax.rem(column, unit)
        is_mean = within >= quarter * modes
        source = jnp.where(is_mean, modes, lax.rem(within, modes))
        pick = (source == lax.broadcasted_iota(jnp.int32, (LANES, depth), 0)).astype(jnp.bfloat16)
        place = jnp.where(within >= quarter * modes, within - quarter * modes, within // modes)
        row = lax.rem(lax.broadcasted_iota(jnp.int32, (tall, 1), 0), rows)
        own = jnp.where(place < quarter, column // unit * quarter + place, -1) == row
        every = jnp.broadcast_to(weights[...][:, None, :], (angles, rows, LANES))
        for part, spread in zip(split(every.reshape(tall, LANES)), (spread_high, spread_low)):
            laid = jnp.dot(part, pick, preferred_element_type=jnp.float32)
            spread[...] = jnp.where(own, laid, 0.0).astype(jnp.bfloat16)

    e_high, e_low = split(eigen[...].reshape(depth, wide))
    estimate = jnp.dot(spread_high[...], e_high, preferred_element_type=jnp.float32)
    estimate += jnp.dot(spread_low[...], e_high, preferred_element_type=jnp.float32)
    estimate += jnp.dot(spread_high[...], e_low, preferred_element_type=jnp.float32)
    floored = jnp.maximum(estimate, floor_value)
    out[...] = proj[...] / floored.reshape(angles, rows, wide)


def correct(projections, eigen, weights, rows, modes):
    angles, _, wide = projections.shape
    ang, pix, unit, _ = eigen.shape
    frame = pl.BlockSpec((angles, rows, wide), lambda q: (0, q, 0))
    return pl.pallas_call(
        functools.partial(correct_kernel, rows, modes),
        grid=(pix,),
        out_shape=jax.ShapeDtypeStruct(projections.shape, jnp.float32),
        in_specs=[
            frame,
            pl.BlockSpec((ang, 1, unit, wide), lambda q: (0, q, 0, 0)),
            pl.BlockSpec((angles, LANES), lambda q: (0, 0)),
        ],
        out_specs=frame,
        scratch_shapes=[pltpu.VMEM((angles * rows, ang * unit), jnp.bfloat16)] * 2,
        compiler_params=pltpu.CompilerParams(vmem_limit_bytes=VMEM_LIMIT),
        name="correct",
    )(projections, eigen, weights)


def inverse_factor(matrix):
    order = matrix.shape[0]
    side = 64
    place = lax.broadcasted_iota(jnp.int32, (order, order), 0)
    other = lax.broadcasted_iota(jnp.int32, (order, order), 1)
    unit = (place == other).astype(jnp.float32)
    gap = jnp.zeros((order, side - order), jnp.float32)
    table = jnp.concatenate([matrix, gap, unit, gap], axis=1)
    below = lax.broadcasted_iota(jnp.int32, (order, 1), 0)
    for j in range(order - 1):
        row = table[j:j + 1, :] / table[j:j + 1, j:j + 1]
        table = table - jnp.where(below > j, table[:, j:j + 1], 0.0) * row
    pivots = jnp.sum(table[:, :order] * unit, axis=1, keepdims=True)
    return table[:, side:side + order] / jnp.sqrt(pivots)


def dot_exact(a, b):
    return jnp.dot(a, b, precision=HIGHEST, preferred_element_type=jnp.float32)


def shards(flats, projections, start_basis):
    rows_dev, cols_dev = flats.shape[1:]
    ang, pix = lax.axis_size("ang"), lax.axis_size("pix")
    npix = rows_dev * cols_dev * ang * pix
    gram = gram_of(flats, ang, pix)
    eigen, weights = fit_weights(flats, projections, gram, start_basis, ang, pix, npix)
    return correct(projections, eigen, weights, rows_dev, start_basis.shape[1])


def solution(mesh):
    in_specs = (P(None, "pix", "ang"), P("ang", None, "pix"), P())
    out_specs = P("ang", None, "pix")
    return jax.shard_map(shards, mesh=mesh, in_specs=in_specs, out_specs=out_specs, check_vma=False)
```
